32 devices in a mesh: group: 4 (over y, core), tile: 8 (over z, x).
Axes of the slice: x: 2, y: 2, z: 4, core: 2. Of those that a mesh axis runs over, the one named last changes fastest.
Arguments:
- embeddings: bfloat16 [12288, 768], P(('group', 'tile')), may hold values from -15 to 15
- clusters: int32 [12288], P(('group', 'tile')), may hold values from 0 to 15, as said below
- cluster_owner: int32 [16], replicated, may hold values from 0 to 3, as said below
Outputs:
- neighbours: bfloat16 [12288, 768], P(('group', 'tile'))
- log_mass: float32 [12288], P(('group', 'tile'))
The draws below stay inside these ranges and needn't reach their ends.
Inputs may be any that keep to these rules, and one draw needn't show every extreme that they name: Among the 384 rows of one device at most 144 belong to clusters of any one group; in every draw one group has exactly 144 rows on every device. `cluster_owner`: each group owns exactly 4 clusters.
All inputs are finite; a program needn't handle non-finite values.
Results may differ from the reference program's by a relative error of at most 0.034.
Values may be sent and summed in bfloat16 or wider, within the bound.
A program may use at most 128 MiB of HBM per device.

```python
import math
import jax
import jax.numpy as jnp
from jax import lax

D = 768
ROW_DEV = 384
CPG = 4
GROUPS = 4
CAP = 144
SLOTS = 576
ROWS = 12288
CLUSTERS = 16


def layout(base_key):
    perm_key, pref_key, full_key, score_key, rows_key, pick_key = jax.random.split(base_key, 6)
    labels = jax.random.permutation(perm_key, CLUSTERS).astype(jnp.int32)
    owners = labels % GROUPS
    members = jnp.argsort(labels, stable=True).astype(jnp.int32)
    prefer = jax.random.randint(pref_key, (GROUPS,), 1, 4)
    fullest = jax.random.randint(full_key, (), 0, GROUPS)
    blocks = ROWS // ROW_DEV
    slot_group = jnp.arange(SLOTS, dtype=jnp.int32) // CAP
    draw_noise = jax.random.randint(score_key, (blocks, SLOTS), 0, 16384)
    ranked = draw_noise * jnp.take(prefer, slot_group)[None, :]
    ranked = jnp.where(slot_group[None, :] == fullest, -1, ranked)
    ranked = ranked * SLOTS + jnp.arange(SLOTS, dtype=jnp.int32)[None, :]
    chosen = jnp.argsort(ranked, axis=1, stable=True)[:, :ROW_DEV].astype(jnp.int32)
    mixing = jax.random.randint(rows_key, (blocks, ROW_DEV), 0, 1048576) * ROW_DEV + jnp.arange(ROW_DEV, dtype=jnp.int32)[None, :]
    order_rows = jnp.argsort(mixing, axis=1, stable=True)
    slot_ids = jnp.take_along_axis(chosen, order_rows, axis=1)
    dest_group = slot_ids // CAP
    pick_index = jax.random.randint(pick_key, (blocks, ROW_DEV), 0, CPG)
    row_clusters = jnp.take(members, dest_group + GROUPS * pick_index)
    return (row_clusters.reshape(ROWS).astype(jnp.int32), owners.astype(jnp.int32))


def draw_clusters(key, part):
    return layout(jax.random.fold_in(key, 7))[0]


def draw_cluster_owner(key, part):
    return layout(jax.random.fold_in(key, 7))[1]


def draw_embeddings(key, part):
    drawn_rows = jax.random.normal(jax.random.fold_in(key, 11), (ROWS, D), jnp.float32)
    return jnp.clip(drawn_rows, -6.0, 6.0).astype(jnp.bfloat16)


def setup_inputs(seed: int = 0) -> dict:
    arg_keys = jax.random.split(jax.random.key(seed), 4)
    embeddings = draw_embeddings(jax.random.fold_in(arg_keys[3], 71), 0)
    clusters = draw_clusters(jax.random.fold_in(arg_keys[3], 71), 0)
    cluster_owner = draw_cluster_owner(jax.random.fold_in(arg_keys[3], 71), 0)
    return {"embeddings": embeddings, "clusters": clusters, "cluster_owner": cluster_owner}


score_scale = 3.0
penalty = 2.0

def block_results(query_rows, query_ids, query_pos, key_rows, key_ids, key_pos):
    products = jnp.dot(query_rows, key_rows.T, preferred_element_type=jnp.float32)
    differs = (query_ids[:, None] != key_ids[None, :]).astype(jnp.float32)
    scores = products * (score_scale / math.sqrt(D)) - penalty * differs
    usable = (key_ids[None, :] >= 0) & (key_pos[None, :] != query_pos[:, None])
    row_peak = lax.optimization_barrier(jnp.max(jnp.where(usable, scores, 0.0), axis=1))
    weights = jnp.exp(jnp.where(usable, scores - row_peak[:, None], -jnp.inf))
    row_total = jnp.exp(-row_peak) + lax.optimization_barrier(jnp.sum(weights, axis=1))
    log_values = row_peak + jnp.log(row_total)
    weighted = jnp.dot(weights.astype(jnp.bfloat16), key_rows, preferred_element_type=jnp.float32)
    return ((weighted / row_total[:, None]).astype(jnp.bfloat16), log_values)

def reference(embeddings, clusters, cluster_owner):
    blocks = ROWS // ROW_DEV
    group_of = jnp.take(cluster_owner, clusters).astype(jnp.int32)
    dest_group = group_of.reshape(blocks, ROW_DEV)
    same_group = dest_group[:, :, None] == dest_group[:, None, :]
    row_index = jnp.arange(ROW_DEV, dtype=jnp.int32)
    earlier = row_index[None, :] < row_index[:, None]
    rank_in = lax.optimization_barrier(jnp.sum(same_group & earlier[None, :, :], axis=2)).astype(jnp.int32)
    source = jnp.broadcast_to(jnp.arange(blocks, dtype=jnp.int32)[:, None], (blocks, ROW_DEV)).reshape(-1)
    flat_dest = dest_group.reshape(-1)
    flat_rank = rank_in.reshape(-1)
    all_rows = jnp.arange(ROWS, dtype=jnp.int32)
    holder = jnp.full((GROUPS, blocks, CAP), -1, dtype=jnp.int32).at[flat_dest, source, flat_rank].set(all_rows)
    group_slots = holder.reshape(GROUPS, blocks * CAP)

    def one_group(key_pos):
        safe_index = jnp.maximum(key_pos, 0)
        key_rows = jnp.take(embeddings, safe_index, axis=0)
        key_ids = jnp.where(key_pos >= 0, jnp.take(clusters, safe_index), -1).astype(jnp.int32)

        def per_block(block_number):
            first_slot = block_number * SLOTS
            query_rows = lax.dynamic_slice_in_dim(key_rows, first_slot, SLOTS, 0)
            query_ids = lax.dynamic_slice_in_dim(key_ids, first_slot, SLOTS, 0)
            query_pos = lax.dynamic_slice_in_dim(key_pos, first_slot, SLOTS, 0)
            return block_results(query_rows, query_ids, query_pos, key_rows, key_ids, key_pos)
        return lax.map(per_block, jnp.arange(blocks * CAP // SLOTS, dtype=jnp.int32))
    mixed, log_values = lax.map(one_group, group_slots)
    flat_mixed = mixed.reshape(GROUPS * blocks * CAP, D)
    flat_log = log_values.reshape(-1)
    where_row = flat_dest * (blocks * CAP) + source * CAP + flat_rank
    return (jnp.take(flat_mixed, where_row, axis=0), jnp.take(flat_log, where_row))
```

```python
import functools
import math

import jax
import jax.numpy as jnp
from jax import lax
from jax.experimental import pallas as pl
from jax.experimental.pallas import tpu as pltpu
from jax.sharding import PartitionSpec as P

MESH = pl.DeviceIdType.MESH
score_scale = 3.0
penalty = 2.0
LOG2E = math.log2(math.e)
LN2 = math.log(2.0)
NEVER = -1e30
SUB = 2


def iota(shape, dim):
    return lax.broadcasted_iota(jnp.int32, shape, dim)


def kernel(
    planes, group_size, cap, lanes, emb_ref, clusters_ref, owner_ref, out_ref, mass_ref,
    keys, ids, queries, query_ids, acc, peak, total, outgoing, out_ids, results, masses, back, back_mass,
    send_sem, recv_sem,
):
    rows, width = emb_ref.shape
    ys = group_size // 2
    members = group_size * SUB
    group_pos = lax.axis_index("group")
    tile_pos = lax.axis_index("tile")
    my_y, my_core = group_pos // 2, group_pos % 2
    my_plane, my_sub = tile_pos // SUB, tile_pos % SUB

    def member(dy, dc, ds):
        return (dy * 2 + dc) * SUB + ds

    def peer(dy, dc, ds):
        y = lax.rem(my_y + dy, ys)
        core = 1 - my_core if dc else my_core
        sub = 1 - my_sub if ds else my_sub
        return (y * 2 + core, my_plane * SUB + sub)

    def plane_of(r):
        place = 0
        bit = 1
        while bit < planes:
            mine = (my_plane // bit) % 2
            place = place + (1 - mine if r & bit else mine) * bit
            bit *= 2
        return place

    def far(r):
        return (group_pos, plane_of(r) * SUB + my_sub)

    everyone = [(dy, dc, ds) for dy in range(ys) for dc in range(2) for ds in range(SUB)][1:]

    barrier = pltpu.get_barrier_semaphore()
    for offset in everyone:
        pl.semaphore_signal(barrier, inc=1, device_id=peer(*offset), device_id_type=MESH)
    for r in range(1, planes):
        pl.semaphore_signal(barrier, inc=1, device_id=far(r), device_id_type=MESH)

    clusters = clusters_ref[...]
    group_row = jnp.zeros_like(clusters)
    for c in range(owner_ref.shape[0]):
        group_row = jnp.where(clusters == c, owner_ref[c], group_row)
    group_row = group_row ^ my_plane
    eye = iota((rows, rows), 0) == iota((rows, rows), 1)
    before = iota((rows, rows), 0) < iota((rows, rows), 1)

    def column(row):
        return jnp.sum(jnp.where(eye, row, 0), axis=1, keepdims=True)

    group_col = column(group_row)
    rank_row = jnp.sum(((group_col == group_row) & before).astype(jnp.int32), axis=0, keepdims=True)
    slot_row = group_row * cap + rank_row
    slot_col = column(slot_row)
    cluster_col = column(clusters)
    placing = (iota((planes * cap, rows), 0) == slot_row).astype(jnp.bfloat16)
    placed = jnp.dot(placing, emb_ref[...], preferred_element_type=jnp.float32).astype(jnp.bfloat16)
    outgoing[...] = placed.reshape(planes, cap, width)
    keys[0, 0] = placed[:cap]
    for r in range(planes):
        lane = iota((rows, lanes), 1)
        here = (lane + r * cap == slot_col) & (lane < cap)
        row = jnp.sum(jnp.where(here, cluster_col + 1, 0), axis=0, keepdims=True) - 1
        out_ids[r] = row
        if r == 0:
            ids[0, 0] = row

    pl.semaphore_wait(barrier, len(everyone) + planes - 1)

    copies = []

    def send(src, dst, to):
        index = len(copies)
        copy = pltpu.make_async_remote_copy(
            src_ref=src, dst_ref=dst, send_sem=send_sem.at[index], recv_sem=recv_sem.at[index],
            device_id=to, device_id_type=MESH,
        )
        copy.start()
        copies.append(copy)
        return copy

    half = (cap // 32 + (1 if cap % 32 else 0)) * 16
    lower, upper = pl.ds(0, half), pl.ds(half, cap - half)

    id_far = [None] + [send(out_ids.at[r], ids.at[0, r], far(r)) for r in range(1, planes)]
    row_far = [None] + [send(outgoing.at[r], keys.at[r, 0], far(r)) for r in range(1, planes)]

    across, along = {}, {}
    last = {r: [] for r in range(planes)}

    def own(r):
        if r:
            row_far[r].wait_recv()
        mine = keys.at[r, 0]
        across[r] = send(mine, keys.at[r, member(0, 0, 1)], peer(0, 0, 1))
        along[r] = [
            send(mine, keys.at[r, member(ys - d, 0, 0)], peer(d, 0, 0)) for d in range(1, ys)
        ]
        last[r].append(send(mine, keys.at[r, member(0, 1, 0)], peer(0, 1, 0)))
        first = (planes - 1 - r) * cap
        queries[first:first + cap, :] = mine[...]

    diagonal = {}

    def forward(r):
        across[r].wait_recv()
        side = keys.at[r, member(0, 0, 1)]
        turned = [
            send(side.at[lower], keys.at[r, member(ys - d, 0, 1)].at[lower], peer(d, 0, 0))
            for d in range(1, ys)
        ]
        last[r].append(send(side, keys.at[r, member(0, 1, 1)], peer(0, 1, 0)))
        crossed = []
        for d in range(1, ys):
            along[r][d - 1].wait_recv()
            side = keys.at[r, member(ys - d, 0, 0)]
            crossed.append(
                send(side.at[upper], keys.at[r, member(ys - d, 0, 1)].at[upper], peer(0, 0, 1))
            )
            last[r].append(send(side, keys.at[r, member(ys - d, 1, 0)], peer(0, 1, 0)))
        diagonal[r] = turned + crossed

    def share(r):
        for copy in diagonal[r]:
            copy.wait_recv()
        for d in range(1, ys):
            last[r].append(
                send(keys.at[r, member(ys - d, 0, 1)], keys.at[r, member(ys - d, 1, 1)], peer(0, 1, 0))
            )

    own(0)
    for r in range(1, planes):
        id_far[r].wait_recv()
    id_near = [
        send(ids.at[0], ids.at[member((ys - dy) % ys, dc, ds)], peer(dy, dc, ds))
        for dy, dc, ds in everyone
    ]
    for r in range(1, planes):
        own(r)
        forward(r - 1)
        if r > 1:
            share(r - 2)

    part = planes * cap // 2
    for r in range(planes):
        first = (planes - 1 - r) * cap
        pick = iota((cap, lanes), 0) == iota((cap, lanes), 1)
        query_ids[first:first + cap, :] = jnp.sum(
            jnp.where(pick, ids[0, r], 0), axis=1, keepdims=True
        )
    acc[...] = jnp.zeros_like(acc)
    peak[...] = jnp.zeros_like(peak)
    total[...] = jnp.ones_like(total)
    for copy in id_near:
        copy.wait_recv()

    def step(r, h):
        start = h * part
        if not isinstance(start, int):
            start = pl.multiple_of(start, 16)
        mine = pl.ds(start, part)
        block = keys[r].reshape(members * cap, width)
        scores = lax.dot_general(
            queries[mine, :], block, (((1,), (1,)), ((), ())), preferred_element_type=jnp.float32
        )
        key_ids = jnp.concatenate([ids[p, r][:, :cap] for p in range(members)], axis=1)
        other = jnp.where(key_ids < 0, NEVER, -penalty * LOG2E)
        bias = jnp.where(query_ids[mine, :] == key_ids, 0.0, other)
        scores = scores * (score_scale * LOG2E / math.sqrt(width)) + bias
        head = scores[:, :lanes]
        lane = iota((part, lanes), 1)
        itself = (iota((part, lanes), 0) - ((planes - 1 - r) * cap - start) == lane) & (lane < cap)
        scores = jnp.concatenate([jnp.where(itself, NEVER, head), scores[:, lanes:]], axis=1)
        old = peak[mine, :]
        new = jnp.maximum(old, jnp.max(scores, axis=1, keepdims=True))
        shrink = jnp.exp2(old - new)
        weights = jnp.exp2(scores - new)
        total[mine, :] = total[mine, :] * shrink + jnp.sum(weights, axis=1, keepdims=True)
        peak[mine, :] = new
        acc[mine, :] = acc[mine, :] * shrink + jnp.dot(
            weights.astype(jnp.bfloat16), block, preferred_element_type=jnp.float32
        )

    def both(r):
        def body(h, carry):
            step(r, h)
            return carry

        lax.fori_loop(0, 2, body, 0)

    def finish(r):
        for copy in last[r]:
            copy.wait_recv()

    for r in range(planes - 2):
        finish(r)
        both(r)
    forward(planes - 1)
    share(planes - 2)
    finish(planes - 2)
    both(planes - 2)
    share(planes - 1)
    finish(planes - 1)

    returned = []
    for h in range(2):
        step(planes - 1, h)
        for spot in range(h * planes // 2, (h + 1) * planes // 2):
            r = planes - 1 - spot
            first = spot * cap
            sums = total[first:first + cap, :]
            results[r] = (acc[first:first + cap, :] / sums).astype(jnp.bfloat16)
            mass = peak[first:first + cap, :] * LN2 + jnp.log(sums)
            pick = iota((cap, lanes), 0) == iota((cap, lanes), 1)
            masses[r] = jnp.sum(jnp.where(pick, mass, 0.0), axis=0, keepdims=True)
            if r:
                returned.append(send(results.at[r], back.at[r], far(r)))
                returned.append(send(masses.at[r], back_mass.at[r], far(r)))
            else:
                back[0] = results[0]
                back_mass[0] = masses[0]
    for copy in returned:
        copy.wait_recv()

    fetch = (iota((rows, planes * cap), 1) == slot_col).astype(jnp.bfloat16)
    found = back[...].reshape(planes * cap, width)
    out_ref[...] = jnp.dot(fetch, found, preferred_element_type=jnp.float32).astype(jnp.bfloat16)
    mass = jnp.zeros((rows, 1), jnp.float32)
    for r in range(planes):
        lane = iota((rows, lanes), 1)
        here = (lane + r * cap == slot_col) & (lane < cap)
        mass = mass + jnp.sum(jnp.where(here, back_mass[r], 0.0), axis=1, keepdims=True)
    mass_ref[...] = jnp.sum(jnp.where(eye, mass, 0.0), axis=0, keepdims=True)
    for copy in copies:
        copy.wait_send()


def per_device(embeddings, clusters, cluster_owner):
    rows, width = embeddings.shape
    group_size = lax.axis_size("group")
    tiles = lax.axis_size("tile")
    planes = tiles // SUB
    assert planes == group_size and planes & (planes - 1) == 0
    most = 3 * rows // (2 * group_size)
    cap = -(-most // 16) * 16
    lanes = -(-cap // 128) * 128
    members = group_size * SUB
    slots = planes * cap
    ys = group_size // 2
    count = 3 * (planes - 1) + planes - 1 + members - 1 + planes * (2 + ys - 1 + 4 * (ys - 1) + 1 + ys)
    vmem = pl.BlockSpec(memory_space=pltpu.VMEM)
    out, mass = pl.pallas_call(
        functools.partial(kernel, planes, group_size, cap, lanes),
        out_shape=(
            jax.ShapeDtypeStruct((rows, width), jnp.bfloat16),
            jax.ShapeDtypeStruct((1, rows), jnp.float32),
        ),
        in_specs=[vmem, vmem, pl.BlockSpec(memory_space=pltpu.SMEM)],
        out_specs=(vmem, vmem),
        scratch_shapes=[
            pltpu.VMEM((planes, members, cap, width), jnp.bfloat16),
            pltpu.VMEM((members, planes, 1, lanes), jnp.int32),
            pltpu.VMEM((slots, width), jnp.bfloat16),
            pltpu.VMEM((slots, 1), jnp.int32),
            pltpu.VMEM((slots, width), jnp.float32),
            pltpu.VMEM((slots, 1), jnp.float32),
            pltpu.VMEM((slots, 1), jnp.float32),
            pltpu.VMEM((planes, cap, width), jnp.bfloat16),
            pltpu.VMEM((planes, 1, lanes), jnp.int32),
            pltpu.VMEM((planes, cap, width), jnp.bfloat16),
            pltpu.VMEM((planes, 1, lanes), jnp.float32),
            pltpu.VMEM((planes, cap, width), jnp.bfloat16),
            pltpu.VMEM((planes, 1, lanes), jnp.float32),
            pltpu.SemaphoreType.DMA((count,)),
            pltpu.SemaphoreType.DMA((count,)),
        ],
        compiler_params=pltpu.CompilerParams(
            collective_id=0, has_side_effects=True, vmem_limit_bytes=48 * 1024 * 1024
        ),
    )(embeddings, clusters.reshape(1, rows), cluster_owner)
    return out, mass.reshape(rows)


def solution(mesh):
    placed = (P(("group", "tile"), None), P(("group", "tile")), P())
    return jax.shard_map(
        per_device,
        mesh=mesh,
        in_specs=placed,
        out_specs=(P(("group", "tile"), None), P(("group", "tile"))),
        check_vma=False,
    )
```

```python
import functools
import math

import jax
import jax.numpy as jnp
from jax import lax
from jax.experimental import pallas as pl
from jax.experimental.pallas import tpu as pltpu
from jax.sharding import PartitionSpec as P

MESH = pl.DeviceIdType.MESH
score_scale = 3.0
penalty = 2.0
LOG2E = math.log2(math.e)
LN2 = math.log(2.0)
NEVER = -1e30
SUB = 2


def iota(shape, dim):
    return lax.broadcasted_iota(jnp.int32, shape, dim)


def kernel(
    planes, group_size, cap, lanes, emb_ref, clusters_ref, owner_ref, out_ref, mass_ref,
    keys, ids, queries, query_ids, acc, peak, total, outgoing, out_ids, results, masses, back, back_mass,
    send_sem, recv_sem,
):
    rows, width = emb_ref.shape
    ys = group_size // 2
    members = group_size * SUB
    group_pos = lax.axis_index("group")
    tile_pos = lax.axis_index("tile")
    my_y, my_core = group_pos // 2, group_pos % 2
    my_plane, my_sub = tile_pos // SUB, tile_pos % SUB

    def member(dy, dc, ds):
        return (dy * 2 + dc) * SUB + ds

    def peer(dy, dc, ds):
        y = lax.rem(my_y + dy, ys)
        core = 1 - my_core if dc else my_core
        sub = 1 - my_sub if ds else my_sub
        return (y * 2 + core, my_plane * SUB + sub)

    def plane_of(r):
        place = 0
        bit = 1
        while bit < planes:
            mine = (my_plane // bit) % 2
            place = place + (1 - mine if r & bit else mine) * bit
            bit *= 2
        return place

    def far(r):
        return (group_pos, plane_of(r) * SUB + my_sub)

    everyone = [(dy, dc, ds) for dy in range(ys) for dc in range(2) for ds in range(SUB)][1:]

    barrier = pltpu.get_barrier_semaphore()
    for offset in everyone:
        pl.semaphore_signal(barrier, inc=1, device_id=peer(*offset), device_id_type=MESH)
    for r in range(1, planes):
        pl.semaphore_signal(barrier, inc=1, device_id=far(r), device_id_type=MESH)

    clusters = clusters_ref[...]
    group_row = jnp.zeros_like(clusters)
    for c in range(owner_ref.shape[0]):
        group_row = jnp.where(clusters == c, owner_ref[c], group_row)
    group_row = group_row ^ my_plane
    eye = iota((rows, rows), 0) == iota((rows, rows), 1)
    before = iota((rows, rows), 0) < iota((rows, rows), 1)

    def column(row):
        return jnp.sum(jnp.where(eye, row, 0), axis=1, keepdims=True)

    group_col = column(group_row)
    rank_row = jnp.sum(((group_col == group_row) & before).astype(jnp.int32), axis=0, keepdims=True)
    slot_row = group_row * cap + rank_row
    slot_col = column(slot_row)
    cluster_col = column(clusters)
    for r in range(planes):
        lane = iota((rows, lanes), 1)
        here = (lane + r * cap == slot_col) & (lane < cap)
        row = jnp.sum(jnp.where(here, cluster_col + 1, 0), axis=0, keepdims=True) - 1
        out_ids[r] = row
        if r == 0:
            ids[0, 0] = row

    pl.semaphore_wait(barrier, len(everyone) + planes - 1)

    copies, gone = [], []

    def send(src, dst, to):
        index = len(copies)
        copy = pltpu.make_async_remote_copy(
            src_ref=src, dst_ref=dst, send_sem=send_sem.at[index], recv_sem=recv_sem.at[index],
            device_id=to, device_id_type=MESH,
        )
        copy.start()
        copies.append(copy)
        return copy

    half = (cap // 32 + (1 if cap % 32 else 0)) * 16
    lower, upper = pl.ds(0, half), pl.ds(half, cap - half)

    def place(r):
        placing = (iota((cap, rows), 0) + r * cap == slot_row).astype(jnp.bfloat16)
        placed = jnp.dot(placing, emb_ref[...], preferred_element_type=jnp.float32)
        return placed.astype(jnp.bfloat16)

    id_far = [None] + [send(out_ids.at[r], ids.at[0, r], far(r)) for r in range(1, planes)]
    row_far = [None]
    for r in range(1, planes):
        outgoing[r] = place(r)
        if r < 3:
            row_far.append(send(outgoing.at[r], keys.at[r, 0], far(r)))
    keys[0, 0] = place(0)

    across, along = {}, {}
    last = {r: [] for r in range(planes)}

    def own(r):
        if r:
            row_far[r].wait_recv()
        mine = keys.at[r, 0]
        across[r] = send(mine, keys.at[r, member(0, 0, 1)], peer(0, 0, 1))
        along[r] = [
            send(mine, keys.at[r, member(ys - d, 0, 0)], peer(d, 0, 0)) for d in range(1, ys)
        ]
        last[r].append(send(mine, keys.at[r, member(0, 1, 0)], peer(0, 1, 0)))
        first = (planes - 1 - r) * cap
        queries[first:first + cap, :] = mine[...]

    diagonal = {}

    def forward(r):
        across[r].wait_recv()
        side = keys.at[r, member(0, 0, 1)]
        turned = [
            send(side.at[lower], keys.at[r, member(ys - d, 0, 1)].at[lower], peer(d, 0, 0))
            for d in range(1, ys)
        ]
        last[r].append(send(side, keys.at[r, member(0, 1, 1)], peer(0, 1, 0)))
        crossed = []
        for d in range(1, ys):
            along[r][d - 1].wait_recv()
            side = keys.at[r, member(ys - d, 0, 0)]
            crossed.append(
                send(side.at[upper], keys.at[r, member(ys - d, 0, 1)].at[upper], peer(0, 0, 1))
            )
            last[r].append(send(side, keys.at[r, member(ys - d, 1, 0)], peer(0, 1, 0)))
        diagonal[r] = turned + crossed

    def share(r):
        for copy in diagonal[r]:
            copy.wait_recv()
        for d in range(1, ys):
            last[r].append(
                send(keys.at[r, member(ys - d, 0, 1)], keys.at[r, member(ys - d, 1, 1)], peer(0, 1, 0))
            )

    part = planes * cap // 2

    def step(r, h):
        start = h * part
        mine = pl.ds(start, part)
        block = keys[r].reshape(members * cap, width)
        scores = lax.dot_general(
            queries[mine, :], block, (((1,), (1,)), ((), ())), preferred_element_type=jnp.float32
        )
        key_ids = jnp.concatenate([ids[p, r][:, :cap] for p in range(members)], axis=1)
        other = jnp.where(key_ids < 0, NEVER, -penalty * LOG2E)
        bias = jnp.where(query_ids[mine, :] == key_ids, 0.0, other)
        scores = scores * (score_scale * LOG2E / math.sqrt(width)) + bias
        head = scores[:, :lanes]
        lane = iota((part, lanes), 1)
        itself = (iota((part, lanes), 0) - ((planes - 1 - r) * cap - start) == lane) & (lane < cap)
        scores = jnp.concatenate([jnp.where(itself, NEVER, head), scores[:, lanes:]], axis=1)
        old = peak[mine, :]
        new = jnp.maximum(old, jnp.max(scores, axis=1, keepdims=True))
        shrink = jnp.exp2(old - new)
        weights = jnp.exp2(scores - new)
        total[mine, :] = total[mine, :] * shrink + jnp.sum(weights, axis=1, keepdims=True)
        peak[mine, :] = new
        acc[mine, :] = acc[mine, :] * shrink + jnp.dot(
            weights.astype(jnp.bfloat16), block, preferred_element_type=jnp.float32
        )

    def finish(r):
        for copy in last[r]:
            copy.wait_recv()

    own(0)
    for r in range(1, planes):
        id_far[r].wait_recv()
    id_near = [
        send(ids.at[0], ids.at[member((ys - dy) % ys, dc, ds)], peer(dy, dc, ds))
        for dy, dc, ds in everyone
    ]
    for r in range(planes):
        first = (planes - 1 - r) * cap
        pick = iota((cap, lanes), 0) == iota((cap, lanes), 1)
        query_ids[first:first + cap, :] = jnp.sum(
            jnp.where(pick, ids[0, r], 0), axis=1, keepdims=True
        )
    acc[...] = jnp.zeros_like(acc)
    peak[...] = jnp.zeros_like(peak)
    total[...] = jnp.ones_like(total)
    near = planes // 2
    waiting = []
    for r in range(planes - 1):
        forward(r)
        own(r + 1)
        if r + 3 < planes:
            row_far[r + 2].wait_send()
            gone.append(row_far[r + 2])
            row_far.append(send(outgoing.at[r + 3], keys.at[r + 3, 0], far(r + 3)))
        if r == 0:
            for copy in id_near:
                copy.wait_recv()
        if r < planes - 2:
            share(r)
        if r + 1 >= near - 1 and r < planes - 2:
            for k in range(len(waiting), r + 1):
                finish(k)
                step(k, 1)
                waiting.append(k)
    for k in waiting:
        step(k, 0)
    share(planes - 2)
    forward(planes - 1)
    for k in range(len(waiting), planes - 1):
        finish(k)
        step(k, 1)
    share(planes - 1)
    for k in range(len(waiting), planes - 1):
        step(k, 0)
    finish(planes - 1)

    returned = []
    for h in range(2):
        step(planes - 1, h)
        for spot in range(h * planes // 2, (h + 1) * planes // 2):
            r = planes - 1 - spot
            first = spot * cap
            sums = total[first:first + cap, :]
            results[r] = (acc[first:first + cap, :] / sums).astype(jnp.bfloat16)
            mass = peak[first:first + cap, :] * LN2 + jnp.log(sums)
            pick = iota((cap, lanes), 0) == iota((cap, lanes), 1)
            masses[r] = jnp.sum(jnp.where(pick, mass, 0.0), axis=0, keepdims=True)
            if r:
                returned.append(send(results.at[r], back.at[r], far(r)))
                returned.append(send(masses.at[r], back_mass.at[r], far(r)))
            else:
                back[0] = results[0]
                back_mass[0] = masses[0]
    for copy in returned:
        copy.wait_recv()

    fetch = (iota((rows, planes * cap), 1) == slot_col).astype(jnp.bfloat16)
    found = back[...].reshape(planes * cap, width)
    out_ref[...] = jnp.dot(fetch, found, preferred_element_type=jnp.float32).astype(jnp.bfloat16)
    mass = jnp.zeros((rows, 1), jnp.float32)
    for r in range(planes):
        lane = iota((rows, lanes), 1)
        here = (lane + r * cap == slot_col) & (lane < cap)
        mass = mass + jnp.sum(jnp.where(here, back_mass[r], 0.0), axis=1, keepdims=True)
    mass_ref[...] = jnp.sum(jnp.where(eye, mass, 0.0), axis=0, keepdims=True)
    for copy in copies:
        if all(copy is not other for other in gone):
            copy.wait_send()


def per_device(embeddings, clusters, cluster_owner):
    rows, width = embeddings.shape
    group_size = lax.axis_size("group")
    tiles = lax.axis_size("tile")
    planes = tiles // SUB
    assert planes == group_size and planes & (planes - 1) == 0
    most = 3 * rows // (2 * group_size)
    cap = -(-most // 16) * 16
    lanes = -(-cap // 128) * 128
    members = group_size * SUB
    slots = planes * cap
    ys = group_size // 2
    count = 3 * (planes - 1) + planes - 1 + members - 1 + planes * (2 + ys - 1 + 4 * (ys - 1) + 1 + ys)
    vmem = pl.BlockSpec(memory_space=pltpu.VMEM)
    out, mass = pl.pallas_call(
        functools.partial(kernel, planes, group_size, cap, lanes),
        out_shape=(
            jax.ShapeDtypeStruct((rows, width), jnp.bfloat16),
            jax.ShapeDtypeStruct((1, rows), jnp.float32),
        ),
        in_specs=[vmem, vmem, pl.BlockSpec(memory_space=pltpu.SMEM)],
        out_specs=(vmem, vmem),
        scratch_shapes=[
            pltpu.VMEM((planes, members, cap, width), jnp.bfloat16),
            pltpu.VMEM((members, planes, 1, lanes), jnp.int32),
            pltpu.VMEM((slots, width), jnp.bfloat16),
            pltpu.VMEM((slots, 1), jnp.int32),
            pltpu.VMEM((slots, width), jnp.float32),
            pltpu.VMEM((slots, 1), jnp.float32),
            pltpu.VMEM((slots, 1), jnp.float32),
            pltpu.VMEM((planes, cap, width), jnp.bfloat16),
            pltpu.VMEM((planes, 1, lanes), jnp.int32),
            pltpu.VMEM((planes, cap, width), jnp.bfloat16),
            pltpu.VMEM((planes, 1, lanes), jnp.float32),
            pltpu.VMEM((planes, cap, width), jnp.bfloat16),
            pltpu.VMEM((planes, 1, lanes), jnp.float32),
            pltpu.SemaphoreType.DMA((count,)),
            pltpu.SemaphoreType.DMA((count,)),
        ],
        compiler_params=pltpu.CompilerParams(
            collective_id=0, has_side_effects=True, vmem_limit_bytes=48 * 1024 * 1024
        ),
    )(embeddings, clusters.reshape(1, rows), cluster_owner)
    return out, mass.reshape(rows)


def solution(mesh):
    placed = (P(("group", "tile"), None), P(("group", "tile")), P())
    return jax.shard_map(
        per_device,
        mesh=mesh,
        in_specs=placed,
        out_specs=(P(("group", "tile"), None), P(("group", "tile"))),
        check_vma=False,
    )
```

```python
import functools
import math

import jax
import jax.numpy as jnp
from jax import lax
from jax.experimental import pallas as pl
from jax.experimental.pallas import tpu as pltpu
from jax.sharding import PartitionSpec as P

MESH = pl.DeviceIdType.MESH
score_scale = 3.0
penalty = 2.0
LOG2E = math.log2(math.e)
LN2 = math.log(2.0)
NEVER = -1e30
SUB = 2


def iota(shape, dim):
    return lax.broadcasted_iota(jnp.int32, shape, dim)


def kernel(
    planes, group_size, cap, lanes, emb_ref, clusters_ref, owner_ref, out_ref, mass_ref,
    keys, ids, queries, query_ids, acc, peak, total, outgoing, out_ids, results, masses, back, back_mass,
    emb, load_sem, send_sem, recv_sem,
):
    rows, width = emb_ref.shape
    load = pltpu.make_async_copy(emb_ref, emb, load_sem)
    load.start()
    ys = group_size // 2
    members = group_size * SUB
    group_pos = lax.axis_index("group")
    tile_pos = lax.axis_index("tile")
    my_y, my_core = group_pos // 2, group_pos % 2
    my_plane, my_sub = tile_pos // SUB, tile_pos % SUB

    straight = [(dy, dc, ds) for dc in range(2) for dy in range(ys) for ds in range(SUB) if not (dy and ds)]
    turning = [(dy, dc, ds) for dc in range(2) for dy in range(ys) for ds in range(SUB) if dy and ds]
    places = straight + turning
    early = len(straight)

    def member(dy, dc, ds):
        return places.index((dy, dc, ds))

    def peer(dy, dc, ds):
        y = lax.rem(my_y + dy, ys)
        core = 1 - my_core if dc else my_core
        sub = 1 - my_sub if ds else my_sub
        return (y * 2 + core, my_plane * SUB + sub)

    def plane_of(r):
        place = 0
        bit = 1
        while bit < planes:
            mine = (my_plane // bit) % 2
            place = place + (1 - mine if r & bit else mine) * bit
            bit *= 2
        return place

    def far(r):
        return (group_pos, plane_of(r) * SUB + my_sub)

    everyone = [(dy, dc, ds) for dy in range(ys) for dc in range(2) for ds in range(SUB)][1:]

    barrier = pltpu.get_barrier_semaphore()
    for offset in everyone:
        pl.semaphore_signal(barrier, inc=1, device_id=peer(*offset), device_id_type=MESH)
    for r in range(1, planes):
        pl.semaphore_signal(barrier, inc=1, device_id=far(r), device_id_type=MESH)

    clusters = clusters_ref[...].reshape(1, rows)
    group_row = jnp.zeros_like(clusters)
    for c in range(owner_ref.shape[0]):
        group_row = jnp.where(clusters == c, owner_ref[c], group_row)
    group_row = group_row ^ my_plane
    eye = iota((rows, rows), 0) == iota((rows, rows), 1)
    before = iota((rows, rows), 0) < iota((rows, rows), 1)

    def column(row):
        return jnp.sum(jnp.where(eye, row, 0), axis=1, keepdims=True)

    group_col = column(group_row)
    rank_row = jnp.sum(((group_col == group_row) & before).astype(jnp.int32), axis=0, keepdims=True)
    slot_row = group_row * cap + rank_row
    slot_col = column(slot_row)
    cluster_col = column(clusters)
    load.wait()
    pl.semaphore_wait(barrier, len(everyone) + planes - 1)

    copies, gone = [], []

    def send(src, dst, to):
        index = len(copies)
        copy = pltpu.make_async_remote_copy(
            src_ref=src, dst_ref=dst, send_sem=send_sem.at[index], recv_sem=recv_sem.at[index],
            device_id=to, device_id_type=MESH,
        )
        copy.start()
        copies.append(copy)
        return copy

    half = (cap // 32 + (1 if cap % 32 else 0)) * 16
    lower, upper = pl.ds(0, half), pl.ds(half, cap - half)

    def place(r):
        placing = (iota((cap, rows), 0) + r * cap == slot_row).astype(jnp.bfloat16)
        placed = jnp.dot(placing, emb[...], preferred_element_type=jnp.float32)
        return placed.astype(jnp.bfloat16)

    across, along = {}, {}
    last = {r: [] for r in range(planes)}

    def own(r):
        if r:
            row_far[r].wait_recv()
        mine = keys.at[r, 0]
        across[r] = send(mine, keys.at[r, member(0, 0, 1)], peer(0, 0, 1))
        along[r] = [
            send(mine, keys.at[r, member(ys - d, 0, 0)], peer(d, 0, 0)) for d in range(1, ys)
        ]
        last[r].append(send(mine, keys.at[r, member(0, 1, 0)], peer(0, 1, 0)))
        first = (planes - 1 - r) * cap
        queries[first:first + cap, :] = mine[...]

    diagonal = {}

    def forward(r):
        across[r].wait_recv()
        side = keys.at[r, member(0, 0, 1)]
        turned = [
            send(side.at[lower], keys.at[r, member(ys - d, 0, 1)].at[lower], peer(d, 0, 0))
            for d in range(1, ys)
        ]
        last[r].append(send(side, keys.at[r, member(0, 1, 1)], peer(0, 1, 0)))
        crossed = []
        for d in range(1, ys):
            along[r][d - 1].wait_recv()
            side = keys.at[r, member(ys - d, 0, 0)]
            crossed.append(
                send(side.at[upper], keys.at[r, member(ys - d, 0, 1)].at[upper], peer(0, 0, 1))
            )
            last[r].append(send(side, keys.at[r, member(ys - d, 1, 0)], peer(0, 1, 0)))
        diagonal[r] = turned + crossed

    tail = {r: [] for r in range(planes)}

    def share(r):
        for copy in diagonal[r]:
            copy.wait_recv()
        for d in range(1, ys):
            tail[r].append(
                send(keys.at[r, member(ys - d, 0, 1)], keys.at[r, member(ys - d, 1, 1)], peer(0, 1, 0))
            )

    def finish(copies_in):
        for copy in copies_in:
            copy.wait_recv()

    def step(r, query_from, query_to, member_from=0, member_to=members):
        start, size = query_from * cap, (query_to - query_from) * cap
        mine = pl.ds(start, size)
        block = keys[r, member_from:member_to].reshape((member_to - member_from) * cap, width)
        scores = lax.dot_general(
            queries[mine, :], block, (((1,), (1,)), ((), ())), preferred_element_type=jnp.float32
        )
        key_ids = jnp.concatenate([ids[p, r][:, :cap] for p in range(member_from, member_to)], axis=1)
        other = jnp.where(key_ids < 0, NEVER, -penalty * LOG2E)
        bias = jnp.where(query_ids[mine, :] == key_ids, 0.0, other)
        scores = scores * (score_scale * LOG2E / math.sqrt(width)) + bias
        spot = planes - 1 - r
        if member_from == 0 and query_from <= spot < query_to:
            head = scores[:, :lanes]
            lane = iota((size, lanes), 1)
            itself = (iota((size, lanes), 0) - (spot * cap - start) == lane) & (lane < cap)
            scores = jnp.concatenate([jnp.where(itself, NEVER, head), scores[:, lanes:]], axis=1)
        old = peak[mine, :]
        new = jnp.maximum(old, jnp.max(scores, axis=1, keepdims=True))
        shrink = jnp.exp2(old - new)
        weights = jnp.exp2(scores - new)
        total[mine, :] = total[mine, :] * shrink + jnp.sum(weights, axis=1, keepdims=True)
        peak[mine, :] = new
        acc[mine, :] = acc[mine, :] * shrink + jnp.dot(
            weights.astype(jnp.bfloat16), block, preferred_element_type=jnp.float32
        )

    keys[0, 0] = place(0)
    own(0)
    row_far = [None]
    for r in range(1, planes):
        outgoing[r] = place(r)
        if r < 3:
            row_far.append(send(outgoing.at[r], keys.at[r, 0], far(r)))
    for r in range(planes):
        lane = iota((rows, lanes), 1)
        here = (lane + r * cap == slot_col) & (lane < cap)
        row = jnp.sum(jnp.where(here, cluster_col + 1, 0), axis=0, keepdims=True) - 1
        out_ids[r] = row
        if r == 0:
            ids[0, 0] = row

    id_far = [send(out_ids.at[r], ids.at[0, r], far(r)) for r in range(1, planes)]
    acc[...] = jnp.zeros_like(acc)
    peak[...] = jnp.zeros_like(peak)
    total[...] = jnp.ones_like(total)
    finish(id_far)
    id_near = [
        send(ids.at[0], ids.at[member((ys - dy) % ys, dc, ds)], peer(dy, dc, ds))
        for dy, dc, ds in everyone
    ]
    for r in range(planes):
        first = (planes - 1 - r) * cap
        pick = iota((cap, lanes), 0) == iota((cap, lanes), 1)
        query_ids[first:first + cap, :] = jnp.sum(
            jnp.where(pick, ids[0, r], 0), axis=1, keepdims=True
        )
    final = planes - 1
    for r in range(final):
        forward(r)
        own(r + 1)
        if r + 3 < planes:
            row_far[r + 2].wait_send()
            gone.append(row_far[r + 2])
            row_far.append(send(outgoing.at[r + 3], keys.at[r + 3, 0], far(r + 3)))
        if r == 0:
            finish(id_near)
        if r + 1 < final - 1:
            share(r)
            finish(last[r] + tail[r])
        elif r + 1 == final - 1:
            for k in range(r):
                step(k, 1, planes)
            share(r)
            finish(last[r] + tail[r])
            step(r, 1, planes)
    for k in range(final - 1):
        step(k, 0, 1)
    share(final - 1)
    finish(last[final - 1] + tail[final - 1])
    middle = planes // 2
    step(final - 1, 0, middle)
    forward(final)
    step(final - 1, middle, planes)
    finish(last[final])
    step(final, middle, planes, 0, early)
    share(final)
    step(final, 0, middle, 0, early)
    finish(tail[final])

    returned = [None] * planes
    for spot in range(planes):
        step(final, spot, spot + 1, early, members)
        r = final - spot
        first = spot * cap
        sums = total[first:first + cap, :]
        results[r] = (acc[first:first + cap, :] / sums).astype(jnp.bfloat16)
        mass = peak[first:first + cap, :] * LN2 + jnp.log(sums)
        pick = iota((cap, lanes), 0) == iota((cap, lanes), 1)
        masses[r] = jnp.sum(jnp.where(pick, mass, 0.0), axis=0, keepdims=True)
        if r:
            returned[r] = [
                send(results.at[r], back.at[r], far(r)), send(masses.at[r], back_mass.at[r], far(r))
            ]
    found = jnp.zeros((rows, width), jnp.float32)
    mass = jnp.zeros((rows, 1), jnp.float32)
    for r in range(planes):
        lane = iota((rows, lanes), 1)
        here = (lane + r * cap == slot_col) & (lane < cap)
        fetch = (iota((rows, cap), 1) + r * cap == slot_col).astype(jnp.bfloat16)
        if r:
            finish(returned[r])
            block, block_mass = back[r], back_mass[r]
        else:
            block, block_mass = results[0], masses[0]
        found = found + jnp.dot(fetch, block, preferred_element_type=jnp.float32)
        mass = mass + jnp.sum(jnp.where(here, block_mass, 0.0), axis=1, keepdims=True)
    out_ref[...] = found.astype(jnp.bfloat16)
    mass_ref[...] = jnp.sum(jnp.where(eye, mass, 0.0), axis=0)
    for copy in copies:
        if all(copy is not other for other in gone):
            copy.wait_send()


def per_device(embeddings, clusters, cluster_owner):
    rows, width = embeddings.shape
    group_size = lax.axis_size("group")
    tiles = lax.axis_size("tile")
    planes = tiles // SUB
    assert planes == group_size and planes & (planes - 1) == 0
    most = 3 * rows // (2 * group_size)
    cap = -(-most // 16) * 16
    lanes = -(-cap // 128) * 128
    members = group_size * SUB
    slots = planes * cap
    ys = group_size // 2
    count = 3 * (planes - 1) + planes - 1 + members - 1 + planes * (2 + ys - 1 + 4 * (ys - 1) + 1 + ys)
    vmem = pl.BlockSpec(memory_space=pltpu.VMEM)
    out, mass = pl.pallas_call(
        functools.partial(kernel, planes, group_size, cap, lanes),
        out_shape=(
            jax.ShapeDtypeStruct((rows, width), jnp.bfloat16),
            jax.ShapeDtypeStruct((rows,), jnp.float32),
        ),
        in_specs=[pl.BlockSpec(memory_space=pl.ANY), vmem, pl.BlockSpec(memory_space=pltpu.SMEM)],
        out_specs=(vmem, vmem),
        scratch_shapes=[
            pltpu.VMEM((planes, members, cap, width), jnp.bfloat16),
            pltpu.VMEM((members, planes, 1, lanes), jnp.int32),
            pltpu.VMEM((slots, width), jnp.bfloat16),
            pltpu.VMEM((slots, 1), jnp.int32),
            pltpu.VMEM((slots, width), jnp.float32),
            pltpu.VMEM((slots, 1), jnp.float32),
            pltpu.VMEM((slots, 1), jnp.float32),
            pltpu.VMEM((planes, cap, width), jnp.bfloat16),
            pltpu.VMEM((planes, 1, lanes), jnp.int32),
            pltpu.VMEM((planes, cap, width), jnp.bfloat16),
            pltpu.VMEM((planes, 1, lanes), jnp.float32),
            pltpu.VMEM((planes, cap, width), jnp.bfloat16),
            pltpu.VMEM((planes, 1, lanes), jnp.float32),
            pltpu.VMEM((rows, width), jnp.bfloat16),
            pltpu.SemaphoreType.DMA,
            pltpu.SemaphoreType.DMA((count,)),
            pltpu.SemaphoreType.DMA((count,)),
        ],
        compiler_params=pltpu.CompilerParams(
            collective_id=0, has_side_effects=True, vmem_limit_bytes=63 * 1024 * 1024
        ),
    )(embeddings, clusters, cluster_owner)
    return out, mass


def solution(mesh):
    placed = (P(("group", "tile"), None), P(("group", "tile")), P())
    return jax.shard_map(
        per_device,
        mesh=mesh,
        in_specs=placed,
        out_specs=(P(("group", "tile"), None), P(("group", "tile"))),
        check_vma=False,
    )
```

```python
import functools
import math

import jax
import jax.numpy as jnp
from jax import lax
from jax.experimental import pallas as pl
from jax.experimental.pallas import tpu as pltpu
from jax.sharding import PartitionSpec as P

MESH = pl.DeviceIdType.MESH
score_scale = 3.0
penalty = 2.0
LOG2E = math.log2(math.e)
LN2 = math.log(2.0)
NEVER = -1e30
SUB = 2


def iota(shape, dim):
    return lax.broadcasted_iota(jnp.int32, shape, dim)


def kernel(
    planes, group_size, cap, lanes, emb_ref, clusters_ref, owner_ref, out_ref, mass_ref,
    keys, ids, queries, query_ids, acc, peak, total, outgoing, out_ids, results, masses, back, back_mass,
    send_sem, recv_sem,
):
    rows, width = emb_ref.shape
    ys = group_size // 2
    members = group_size * SUB
    group_pos = lax.axis_index("group")
    tile_pos = lax.axis_index("tile")
    my_y, my_core = group_pos // 2, group_pos % 2
    my_plane, my_sub = tile_pos // SUB, tile_pos % SUB

    straight = [(dy, dc, ds) for dc in range(2) for dy in range(ys) for ds in range(SUB) if not (dy and ds)]
    turning = [(dy, dc, ds) for dc in range(2) for dy in range(ys) for ds in range(SUB) if dy and ds]
    places = straight + turning
    early = len(straight)

    def member(dy, dc, ds):
        return places.index((dy, dc, ds))

    def peer(dy, dc, ds):
        y = lax.rem(my_y + dy, ys)
        core = 1 - my_core if dc else my_core
        sub = 1 - my_sub if ds else my_sub
        return (y * 2 + core, my_plane * SUB + sub)

    def plane_of(r):
        place = 0
        bit = 1
        while bit < planes:
            mine = (my_plane // bit) % 2
            place = place + (1 - mine if r & bit else mine) * bit
            bit *= 2
        return place

    def far(r):
        return (group_pos, plane_of(r) * SUB + my_sub)

    everyone = [(dy, dc, ds) for dy in range(ys) for dc in range(2) for ds in range(SUB)][1:]

    barrier = pltpu.get_barrier_semaphore()
    for offset in everyone:
        pl.semaphore_signal(barrier, inc=1, device_id=peer(*offset), device_id_type=MESH)
    for r in range(1, planes):
        pl.semaphore_signal(barrier, inc=1, device_id=far(r), device_id_type=MESH)

    clusters = clusters_ref[...].reshape(1, rows)
    group_row = jnp.zeros_like(clusters)
    for c in range(owner_ref.shape[0]):
        group_row = jnp.where(clusters == c, owner_ref[c], group_row)
    group_row = group_row ^ my_plane
    eye = iota((rows, rows), 0) == iota((rows, rows), 1)
    before = iota((rows, rows), 0) < iota((rows, rows), 1)

    def column(row):
        return jnp.sum(jnp.where(eye, row, 0), axis=1, keepdims=True)

    group_col = column(group_row)
    rank_row = jnp.sum(((group_col == group_row) & before).astype(jnp.int32), axis=0, keepdims=True)
    slot_row = group_row * cap + rank_row
    slot_col = column(slot_row)
    cluster_col = column(clusters)
    pl.semaphore_wait(barrier, len(everyone) + planes - 1)

    copies, gone = [], []

    def send(src, dst, to):
        index = len(copies)
        copy = pltpu.make_async_remote_copy(
            src_ref=src, dst_ref=dst, send_sem=send_sem.at[index], recv_sem=recv_sem.at[index],
            device_id=to, device_id_type=MESH,
        )
        copy.start()
        copies.append(copy)
        return copy

    half = (cap // 32 + (1 if cap % 32 else 0)) * 16
    lower, upper = pl.ds(0, half), pl.ds(half, cap - half)

    def place(r):
        placing = (iota((cap, rows), 0) + r * cap == slot_row).astype(jnp.bfloat16)
        placed = jnp.dot(placing, emb_ref[...], preferred_element_type=jnp.float32)
        return placed.astype(jnp.bfloat16)

    across, along = {}, {}
    last = {r: [] for r in range(planes)}

    def own(r):
        if r:
            row_far[r].wait_recv()
        mine = keys.at[r, 0]
        across[r] = send(mine, keys.at[r, member(0, 0, 1)], peer(0, 0, 1))
        along[r] = [
            send(mine, keys.at[r, member(ys - d, 0, 0)], peer(d, 0, 0)) for d in range(1, ys)
        ]
        last[r].append(send(mine, keys.at[r, member(0, 1, 0)], peer(0, 1, 0)))
        first = (planes - 1 - r) * cap
        queries[first:first + cap, :] = mine[...]

    diagonal = {}

    def forward(r):
        across[r].wait_recv()
        side = keys.at[r, member(0, 0, 1)]
        turned = [
            send(side.at[lower], keys.at[r, member(ys - d, 0, 1)].at[lower], peer(d, 0, 0))
            for d in range(1, ys)
        ]
        last[r].append(send(side, keys.at[r, member(0, 1, 1)], peer(0, 1, 0)))
        crossed = []
        for d in range(1, ys):
            along[r][d - 1].wait_recv()
            side = keys.at[r, member(ys - d, 0, 0)]
            crossed.append(
                send(side.at[upper], keys.at[r, member(ys - d, 0, 1)].at[upper], peer(0, 0, 1))
            )
            last[r].append(send(side, keys.at[r, member(ys - d, 1, 0)], peer(0, 1, 0)))
        diagonal[r] = turned + crossed

    tail = {r: [] for r in range(planes)}

    def share(r):
        for copy in diagonal[r]:
            copy.wait_recv()
        for d in range(1, ys):
            tail[r].append(
                send(keys.at[r, member(ys - d, 0, 1)], keys.at[r, member(ys - d, 1, 1)], peer(0, 1, 0))
            )

    def finish(copies_in):
        for copy in copies_in:
            copy.wait_recv()

    def step(r, query_from, query_to, member_from=0, member_to=members):
        start, size = query_from * cap, (query_to - query_from) * cap
        mine = pl.ds(start, size)
        block = keys[r, member_from:member_to].reshape((member_to - member_from) * cap, width)
        scores = lax.dot_general(
            queries[mine, :], block, (((1,), (1,)), ((), ())), preferred_element_type=jnp.float32
        )
        key_ids = jnp.concatenate([ids[p, r][:, :cap] for p in range(member_from, member_to)], axis=1)
        other = jnp.where(key_ids < 0, NEVER, -penalty * LOG2E)
        bias = jnp.where(query_ids[mine, :] == key_ids, 0.0, other)
        scores = scores * (score_scale * LOG2E / math.sqrt(width)) + bias
        spot = planes - 1 - r
        if member_from == 0 and query_from <= spot < query_to:
            head = scores[:, :lanes]
            lane = iota((size, lanes), 1)
            itself = (iota((size, lanes), 0) - (spot * cap - start) == lane) & (lane < cap)
            scores = jnp.concatenate([jnp.where(itself, NEVER, head), scores[:, lanes:]], axis=1)
        old = peak[mine, :]
        new = jnp.maximum(old, jnp.max(scores, axis=1, keepdims=True))
        shrink = jnp.exp2(old - new)
        weights = jnp.exp2(scores - new)
        total[mine, :] = total[mine, :] * shrink + jnp.sum(weights, axis=1, keepdims=True)
        peak[mine, :] = new
        acc[mine, :] = acc[mine, :] * shrink + jnp.dot(
            weights.astype(jnp.bfloat16), block, preferred_element_type=jnp.float32
        )

    keys[0, 0] = place(0)
    own(0)
    row_far = [None]
    for r in range(1, planes):
        outgoing[r] = place(r)
        if r < 3:
            row_far.append(send(outgoing.at[r], keys.at[r, 0], far(r)))
    for r in range(planes):
        lane = iota((rows, lanes), 1)
        here = (lane + r * cap == slot_col) & (lane < cap)
        row = jnp.sum(jnp.where(here, cluster_col + 1, 0), axis=0, keepdims=True) - 1
        out_ids[r] = row
        if r == 0:
            ids[0, 0] = row

    id_far = [send(out_ids.at[r], ids.at[0, r], far(r)) for r in range(1, planes)]
    acc[...] = jnp.zeros_like(acc)
    peak[...] = jnp.zeros_like(peak)
    total[...] = jnp.ones_like(total)
    finish(id_far)
    id_near = [
        send(ids.at[0], ids.at[member((ys - dy) % ys, dc, ds)], peer(dy, dc, ds))
        for dy, dc, ds in everyone
    ]
    for r in range(planes):
        first = (planes - 1 - r) * cap
        pick = iota((cap, lanes), 0) == iota((cap, lanes), 1)
        query_ids[first:first + cap, :] = jnp.sum(
            jnp.where(pick, ids[0, r], 0), axis=1, keepdims=True
        )
    final, middle = planes - 1, planes // 2
    scored = 0
    for r in range(final - 1):
        own(r + 1)
        forward(r)
        if r + 3 < planes:
            row_far[r + 2].wait_send()
            gone.append(row_far[r + 2])
            row_far.append(send(outgoing.at[r + 3], keys.at[r + 3, 0], far(r + 3)))
        if r == 0:
            finish(id_near)
            continue
        share(r - 1)
        if r + 1 >= middle:
            for k in range(scored, r):
                finish(last[k] + tail[k])
                step(k, middle, planes)
            scored = r
    forward(final - 1)
    share(final - 2)
    finish(last[final - 2] + tail[final - 2])
    step(final - 2, middle, planes)
    own(final)
    for k in range(final - 1):
        step(k, 0, middle)
        if k == 0:
            share(final - 1)
    forward(final)
    finish(last[final - 1] + tail[final - 1])
    step(final - 1, middle, planes)
    share(final)
    step(final - 1, 0, middle)
    finish(last[final] + tail[final])

    returned = [None] * planes
    for spot in range(planes):
        if spot == 0:
            step(final, 0, middle)
        elif spot == middle:
            step(final, middle, planes)
        r = final - spot
        first = spot * cap
        sums = total[first:first + cap, :]
        results[r] = (acc[first:first + cap, :] / sums).astype(jnp.bfloat16)
        mass = peak[first:first + cap, :] * LN2 + jnp.log(sums)
        pick = iota((cap, lanes), 0) == iota((cap, lanes), 1)
        masses[r] = jnp.sum(jnp.where(pick, mass, 0.0), axis=0, keepdims=True)
        if r:
            returned[r] = [
                send(results.at[r], back.at[r], far(r)), send(masses.at[r], back_mass.at[r], far(r))
            ]
    found = jnp.zeros((rows, width), jnp.float32)
    mass = jnp.zeros((rows, 1), jnp.float32)
    for r in range(planes):
        lane = iota((rows, lanes), 1)
        here = (lane + r * cap == slot_col) & (lane < cap)
        fetch = (iota((rows, cap), 1) + r * cap == slot_col).astype(jnp.bfloat16)
        if r:
            finish(returned[r])
            block, block_mass = back[r], back_mass[r]
        else:
            block, block_mass = results[0], masses[0]
        found = found + jnp.dot(fetch, block, preferred_element_type=jnp.float32)
        mass = mass + jnp.sum(jnp.where(here, block_mass, 0.0), axis=1, keepdims=True)
    out_ref[...] = found.astype(jnp.bfloat16)
    mass_ref[...] = jnp.sum(jnp.where(eye, mass, 0.0), axis=0)
    for copy in copies:
        if all(copy is not other for other in gone):
            copy.wait_send()


def per_device(embeddings, clusters, cluster_owner):
    rows, width = embeddings.shape
    group_size = lax.axis_size("group")
    tiles = lax.axis_size("tile")
    planes = tiles // SUB
    assert planes == group_size and planes & (planes - 1) == 0
    most = 3 * rows // (2 * group_size)
    cap = -(-most // 16) * 16
    lanes = -(-cap // 128) * 128
    members = group_size * SUB
    slots = planes * cap
    ys = group_size // 2
    count = 3 * (planes - 1) + planes - 1 + members - 1 + planes * (2 + ys - 1 + 4 * (ys - 1) + 1 + ys)
    vmem = pl.BlockSpec(memory_space=pltpu.VMEM)
    out, mass = pl.pallas_call(
        functools.partial(kernel, planes, group_size, cap, lanes),
        out_shape=(
            jax.ShapeDtypeStruct((rows, width), jnp.bfloat16),
            jax.ShapeDtypeStruct((rows,), jnp.float32),
        ),
        in_specs=[vmem, vmem, pl.BlockSpec(memory_space=pltpu.SMEM)],
        out_specs=(vmem, vmem),
        scratch_shapes=[
            pltpu.VMEM((planes, members, cap, width), jnp.bfloat16),
            pltpu.VMEM((members, planes, 1, lanes), jnp.int32),
            pltpu.VMEM((slots, width), jnp.bfloat16),
            pltpu.VMEM((slots, 1), jnp.int32),
            pltpu.VMEM((slots, width), jnp.float32),
            pltpu.VMEM((slots, 1), jnp.float32),
            pltpu.VMEM((slots, 1), jnp.float32),
            pltpu.VMEM((planes, cap, width), jnp.bfloat16),
            pltpu.VMEM((planes, 1, lanes), jnp.int32),
            pltpu.VMEM((planes, cap, width), jnp.bfloat16),
            pltpu.VMEM((planes, 1, lanes), jnp.float32),
            pltpu.VMEM((planes, cap, width), jnp.bfloat16),
            pltpu.VMEM((planes, 1, lanes), jnp.float32),
            pltpu.SemaphoreType.DMA((count,)),
            pltpu.SemaphoreType.DMA((count,)),
        ],
        compiler_params=pltpu.CompilerParams(
            collective_id=0, has_side_effects=True, vmem_limit_bytes=48 * 1024 * 1024
        ),
    )(embeddings, clusters, cluster_owner)
    return out, mass


def solution(mesh):
    placed = (P(("group", "tile"), None), P(("group", "tile")), P())
    return jax.shard_map(
        per_device,
        mesh=mesh,
        in_specs=placed,
        out_specs=(P(("group", "tile"), None), P(("group", "tile"))),
        check_vma=False,
    )
```

```python
import functools
import math

import jax
import jax.numpy as jnp
from jax import lax
from jax.experimental import pallas as pl
from jax.experimental.pallas import tpu as pltpu
from jax.sharding import PartitionSpec as P

MESH = pl.DeviceIdType.MESH
score_scale = 3.0
penalty = 2.0
LOG2E = math.log2(math.e)
LN2 = math.log(2.0)
NEVER = -1e30
SUB = 2


def iota(shape, dim):
    return lax.broadcasted_iota(jnp.int32, shape, dim)


def kernel(
    planes, group_size, cap, lanes, emb_ref, clusters_ref, owner_ref, out_ref, mass_ref,
    keys, ids, queries, query_ids, acc, peak, total, outgoing, out_ids, results, masses, back, back_mass,
    send_sem, recv_sem,
):
    rows, width = emb_ref.shape
    ys = group_size // 2
    members = group_size * SUB
    group_pos = lax.axis_index("group")
    tile_pos = lax.axis_index("tile")
    my_y, my_core = group_pos // 2, group_pos % 2
    my_plane, my_sub = tile_pos // SUB, tile_pos % SUB

    straight = [(dy, dc, ds) for dc in range(2) for dy in range(ys) for ds in range(SUB) if not (dy and ds)]
    turning = [(dy, dc, ds) for dc in range(2) for dy in range(ys) for ds in range(SUB) if dy and ds]
    places = straight + turning
    early = len(straight)

    def member(dy, dc, ds):
        return places.index((dy, dc, ds))

    def peer(dy, dc, ds):
        y = lax.rem(my_y + dy, ys)
        core = 1 - my_core if dc else my_core
        sub = 1 - my_sub if ds else my_sub
        return (y * 2 + core, my_plane * SUB + sub)

    def plane_of(r):
        place = 0
        bit = 1
        while bit < planes:
            mine = (my_plane // bit) % 2
            place = place + (1 - mine if r & bit else mine) * bit
            bit *= 2
        return place

    def far(r):
        return (group_pos, plane_of(r) * SUB + my_sub)

    everyone = [(dy, dc, ds) for dy in range(ys) for dc in range(2) for ds in range(SUB)][1:]

    barrier = pltpu.get_barrier_semaphore()
    for offset in everyone:
        pl.semaphore_signal(barrier, inc=1, device_id=peer(*offset), device_id_type=MESH)
    for r in range(1, planes):
        pl.semaphore_signal(barrier, inc=1, device_id=far(r), device_id_type=MESH)

    clusters = clusters_ref[...]
    group_row = jnp.zeros_like(clusters)
    for c in range(owner_ref.shape[0]):
        group_row = jnp.where(clusters == c, owner_ref[c], group_row)
    group_row = group_row ^ my_plane
    eye = iota((rows, rows), 0) == iota((rows, rows), 1)
    before = iota((rows, rows), 0) < iota((rows, rows), 1)

    def column(row):
        return jnp.sum(jnp.where(eye, row, 0), axis=1, keepdims=True)

    group_col = column(group_row)
    rank_row = jnp.sum(((group_col == group_row) & before).astype(jnp.int32), axis=0, keepdims=True)
    slot_row = group_row * cap + rank_row
    slot_col = column(slot_row)
    cluster_col = column(clusters)
    pl.semaphore_wait(barrier, len(everyone) + planes - 1)

    copies = []

    def send(src, dst, to):
        index = len(copies)
        copy = pltpu.make_async_remote_copy(
            src_ref=src, dst_ref=dst, send_sem=send_sem.at[index], recv_sem=recv_sem.at[index],
            device_id=to, device_id_type=MESH,
        )
        copy.start()
        copies.append(copy)
        return copy

    half = (cap // 32 + (1 if cap % 32 else 0)) * 16
    lower, upper = pl.ds(0, half), pl.ds(half, cap - half)

    def place(r):
        placing = (iota((cap, rows), 0) + r * cap == slot_row).astype(jnp.bfloat16)
        placed = jnp.dot(placing, emb_ref[...], preferred_element_type=jnp.float32)
        return placed.astype(jnp.bfloat16)

    across, along = {}, {}
    last = {r: [] for r in range(planes)}

    def own(r):
        if r:
            row_far[r].wait_recv()
        mine = keys.at[r, 0]
        across[r] = send(mine, keys.at[r, member(0, 0, 1)], peer(0, 0, 1))
        along[r] = [
            send(mine, keys.at[r, member(ys - d, 0, 0)], peer(d, 0, 0)) for d in range(1, ys)
        ]
        last[r].append(send(mine, keys.at[r, member(0, 1, 0)], peer(0, 1, 0)))
        first = (planes - 1 - r) * cap
        queries[first:first + cap, :] = mine[...]

    diagonal = {}

    def forward(r):
        across[r].wait_recv()
        side = keys.at[r, member(0, 0, 1)]
        turned = [
            send(side.at[lower], keys.at[r, member(ys - d, 0, 1)].at[lower], peer(d, 0, 0))
            for d in range(1, ys)
        ]
        last[r].append(send(side, keys.at[r, member(0, 1, 1)], peer(0, 1, 0)))
        crossed = []
        for d in range(1, ys):
            along[r][d - 1].wait_recv()
            side = keys.at[r, member(ys - d, 0, 0)]
            crossed.append(
                send(side.at[upper], keys.at[r, member(ys - d, 0, 1)].at[upper], peer(0, 0, 1))
            )
            last[r].append(send(side, keys.at[r, member(ys - d, 1, 0)], peer(0, 1, 0)))
        diagonal[r] = turned + crossed

    tail = {r: [] for r in range(planes)}

    def share(r):
        for copy in diagonal[r]:
            copy.wait_recv()
        for d in range(1, ys):
            tail[r].append(
                send(keys.at[r, member(ys - d, 0, 1)], keys.at[r, member(ys - d, 1, 1)], peer(0, 1, 0))
            )

    def finish(copies_in):
        for copy in copies_in:
            copy.wait_recv()

    def step(r, query_from, query_to, member_from=0, member_to=members):
        start, size = query_from * cap, (query_to - query_from) * cap
        mine = pl.ds(start, size)
        block = keys[r, member_from:member_to].reshape((member_to - member_from) * cap, width)
        scores = lax.dot_general(
            queries[mine, :], block, (((1,), (1,)), ((), ())), preferred_element_type=jnp.float32
        )
        key_ids = jnp.concatenate([ids[p, r][:, :cap] for p in range(member_from, member_to)], axis=1)
        other = jnp.where(key_ids < 0, NEVER, -penalty * LOG2E)
        bias = jnp.where(query_ids[mine, :] == key_ids, 0.0, other)
        scores = scores * (score_scale * LOG2E / math.sqrt(width)) + bias
        spot = planes - 1 - r
        if member_from == 0 and query_from <= spot < query_to:
            head = scores[:, :lanes]
            lane = iota((size, lanes), 1)
            itself = (iota((size, lanes), 0) - (spot * cap - start) == lane) & (lane < cap)
            scores = jnp.concatenate([jnp.where(itself, NEVER, head), scores[:, lanes:]], axis=1)
        old = peak[mine, :]
        new = jnp.maximum(old, jnp.max(scores, axis=1, keepdims=True))
        shrink = jnp.exp2(old - new)
        weights = jnp.exp2(scores - new)
        total[mine, :] = total[mine, :] * shrink + jnp.sum(weights, axis=1, keepdims=True)
        peak[mine, :] = new
        acc[mine, :] = acc[mine, :] * shrink + jnp.dot(
            weights.astype(jnp.bfloat16), block, preferred_element_type=jnp.float32
        )

    for r in range(planes):
        lane = iota((rows, lanes), 1)
        here = (lane + r * cap == slot_col) & (lane < cap)
        row = jnp.sum(jnp.where(here, cluster_col + 1, 0), axis=0, keepdims=True) - 1
        out_ids[r] = row
        if r == 0:
            ids[0, 0] = row

    id_far = [send(out_ids.at[r], ids.at[0, r], far(r)) for r in range(1, planes)]
    row_far = [None]
    for r in range(1, planes):
        outgoing[r] = place(r)
        row_far.append(send(outgoing.at[r], keys.at[r, 0], far(r)))
    keys[0, 0] = place(0)
    own(0)
    acc[...] = jnp.zeros_like(acc)
    peak[...] = jnp.zeros_like(peak)
    total[...] = jnp.ones_like(total)
    finish(id_far)
    id_near = [
        send(ids.at[0], ids.at[member((ys - dy) % ys, dc, ds)], peer(dy, dc, ds))
        for dy, dc, ds in everyone
    ]
    for r in range(planes):
        first = (planes - 1 - r) * cap
        pick = iota((cap, lanes), 0) == iota((cap, lanes), 1)
        query_ids[first:first + cap, :] = jnp.sum(
            jnp.where(pick, ids[0, r], 0), axis=1, keepdims=True
        )
    final, middle = planes - 1, planes // 2
    forward(0)
    own(1)
    share(0)
    finish(id_near)
    for r in range(2, planes):
        own(r)
        forward(r - 1)
        if r == middle:
            finish(last[0] + tail[0])
            step(0, middle, planes)
        if r > 2:
            share(r - 2)
    step(0, 0, middle)
    for k in range(1, final - 1):
        finish(last[k] + tail[k])
        step(k, middle, planes)
        if k == 1:
            forward(final)
        step(k, 0, middle)
    share(final - 1)
    finish(last[final - 1] + tail[final - 1])
    step(final - 1, middle, planes)
    share(final)
    step(final - 1, 0, middle)
    finish(last[final] + tail[final])

    returned = [None] * planes
    for spot in range(planes):
        if spot == 0:
            step(final, 0, middle)
        elif spot == middle:
            step(final, middle, planes)
        r = final - spot
        first = spot * cap
        sums = total[first:first + cap, :]
        results[r] = (acc[first:first + cap, :] / sums).astype(jnp.bfloat16)
        mass = peak[first:first + cap, :] * LN2 + jnp.log(sums)
        pick = iota((cap, lanes), 0) == iota((cap, lanes), 1)
        masses[r] = jnp.sum(jnp.where(pick, mass, 0.0), axis=0, keepdims=True)
        if r:
            returned[r] = [
                send(results.at[r], back.at[r], far(r)), send(masses.at[r], back_mass.at[r], far(r))
            ]
    found = jnp.zeros((rows, width), jnp.float32)
    mass = jnp.zeros((rows, 1), jnp.float32)
    for r in range(planes):
        lane = iota((rows, lanes), 1)
        here = (lane + r * cap == slot_col) & (lane < cap)
        fetch = (iota((rows, cap), 1) + r * cap == slot_col).astype(jnp.bfloat16)
        if r:
            finish(returned[r])
            block, block_mass = back[r], back_mass[r]
        else:
            block, block_mass = results[0], masses[0]
        found = found + jnp.dot(fetch, block, preferred_element_type=jnp.float32)
        mass = mass + jnp.sum(jnp.where(here, block_mass, 0.0), axis=1, keepdims=True)
    out_ref[...] = found.astype(jnp.bfloat16)
    mass_ref[...] = jnp.sum(jnp.where(eye, mass, 0.0), axis=0, keepdims=True)
    for copy in copies:
        copy.wait_send()


def per_device(embeddings, clusters, cluster_owner):
    rows, width = embeddings.shape
    group_size = lax.axis_size("group")
    tiles = lax.axis_size("tile")
    planes = tiles // SUB
    assert planes == group_size and planes & (planes - 1) == 0
    most = 3 * rows // (2 * group_size)
    cap = -(-most // 16) * 16
    lanes = -(-cap // 128) * 128
    members = group_size * SUB
    slots = planes * cap
    ys = group_size // 2
    count = 3 * (planes - 1) + planes - 1 + members - 1 + planes * (2 + ys - 1 + 4 * (ys - 1) + 1 + ys)
    vmem = pl.BlockSpec(memory_space=pltpu.VMEM)
    out, mass = pl.pallas_call(
        functools.partial(kernel, planes, group_size, cap, lanes),
        out_shape=(
            jax.ShapeDtypeStruct((rows, width), jnp.bfloat16),
            jax.ShapeDtypeStruct((1, rows), jnp.float32),
        ),
        in_specs=[vmem, vmem, pl.BlockSpec(memory_space=pltpu.SMEM)],
        out_specs=(vmem, vmem),
        scratch_shapes=[
            pltpu.VMEM((planes, members, cap, width), jnp.bfloat16),
            pltpu.VMEM((members, planes, 1, lanes), jnp.int32),
            pltpu.VMEM((slots, width), jnp.bfloat16),
            pltpu.VMEM((slots, 1), jnp.int32),
            pltpu.VMEM((slots, width), jnp.float32),
            pltpu.VMEM((slots, 1), jnp.float32),
            pltpu.VMEM((slots, 1), jnp.float32),
            pltpu.VMEM((planes, cap, width), jnp.bfloat16),
            pltpu.VMEM((planes, 1, lanes), jnp.int32),
            pltpu.VMEM((planes, cap, width), jnp.bfloat16),
            pltpu.VMEM((planes, 1, lanes), jnp.float32),
            pltpu.VMEM((planes, cap, width), jnp.bfloat16),
            pltpu.VMEM((planes, 1, lanes), jnp.float32),
            pltpu.SemaphoreType.DMA((count,)),
            pltpu.SemaphoreType.DMA((count,)),
        ],
        compiler_params=pltpu.CompilerParams(
            collective_id=0, has_side_effects=True, vmem_limit_bytes=48 * 1024 * 1024
        ),
    )(embeddings, clusters.reshape(1, rows), cluster_owner)
    return out, mass.reshape(rows)


def solution(mesh):
    placed = (P(("group", "tile"), None), P(("group", "tile")), P())
    return jax.shard_map(
        per_device,
        mesh=mesh,
        in_specs=placed,
        out_specs=(P(("group", "tile"), None), P(("group", "tile"))),
        check_vma=False,
    )
```

```python
import functools
import math

import jax
import jax.numpy as jnp
from jax import lax
from jax.experimental import pallas as pl
from jax.experimental.pallas import tpu as pltpu
from jax.sharding import PartitionSpec as P

MESH = pl.DeviceIdType.MESH
score_scale = 3.0
penalty = 2.0
LOG2E = math.log2(math.e)
LN2 = math.log(2.0)
NEVER = -1e30
SUB = 2


def iota(shape, dim):
    return lax.broadcasted_iota(jnp.int32, shape, dim)


def kernel(
    planes, group_size, cap, lanes, emb_ref, clusters_ref, owner_ref, out_ref, mass_ref,
    keys, ids, queries, query_ids, acc, peak, total, outgoing, out_ids, results, masses, back, back_mass,
    send_sem, recv_sem,
):
    rows, width = emb_ref.shape
    ys = group_size // 2
    members = group_size * SUB
    group_pos = lax.axis_index("group")
    tile_pos = lax.axis_index("tile")
    my_y, my_core = group_pos // 2, group_pos % 2
    my_plane, my_sub = tile_pos // SUB, tile_pos % SUB

    straight = [(dy, dc, ds) for dc in range(2) for dy in range(ys) for ds in range(SUB) if not (dy and ds)]
    turning = [(dy, dc, ds) for dc in range(2) for dy in range(ys) for ds in range(SUB) if dy and ds]
    places = straight + turning
    early = len(straight)

    def member(dy, dc, ds):
        return places.index((dy, dc, ds))

    def peer(dy, dc, ds):
        y = lax.rem(my_y + dy, ys)
        core = 1 - my_core if dc else my_core
        sub = 1 - my_sub if ds else my_sub
        return (y * 2 + core, my_plane * SUB + sub)

    def plane_of(r):
        place = 0
        bit = 1
        while bit < planes:
            mine = (my_plane // bit) % 2
            place = place + (1 - mine if r & bit else mine) * bit
            bit *= 2
        return place

    def far(r):
        return (group_pos, plane_of(r) * SUB + my_sub)

    everyone = [(dy, dc, ds) for dy in range(ys) for dc in range(2) for ds in range(SUB)][1:]

    barrier = pltpu.get_barrier_semaphore()
    for offset in everyone:
        pl.semaphore_signal(barrier, inc=1, device_id=peer(*offset), device_id_type=MESH)
    for r in range(1, planes):
        pl.semaphore_signal(barrier, inc=1, device_id=far(r), device_id_type=MESH)

    clusters = clusters_ref[...]
    group_row = jnp.zeros_like(clusters)
    for c in range(owner_ref.shape[0]):
        group_row = jnp.where(clusters == c, owner_ref[c], group_row)
    group_row = group_row ^ my_plane
    eye = iota((rows, rows), 0) == iota((rows, rows), 1)
    before = iota((rows, rows), 0) < iota((rows, rows), 1)

    def column(row):
        return jnp.sum(jnp.where(eye, row, 0), axis=1, keepdims=True)

    group_col = column(group_row)
    rank_row = jnp.sum(((group_col == group_row) & before).astype(jnp.int32), axis=0, keepdims=True)
    slot_row = group_row * cap + rank_row
    slot_col = column(slot_row)
    cluster_col = column(clusters)
    pl.semaphore_wait(barrier, len(everyone) + planes - 1)

    copies = []

    def send(src, dst, to):
        index = len(copies)
        copy = pltpu.make_async_remote_copy(
            src_ref=src, dst_ref=dst, send_sem=send_sem.at[index], recv_sem=recv_sem.at[index],
            device_id=to, device_id_type=MESH,
        )
        copy.start()
        copies.append(copy)
        return copy

    half = (cap // 32 + (1 if cap % 32 else 0)) * 16
    lower, upper = pl.ds(0, half), pl.ds(half, cap - half)

    def place(r):
        placing = (iota((cap, rows), 0) + r * cap == slot_row).astype(jnp.bfloat16)
        placed = jnp.dot(placing, emb_ref[...], preferred_element_type=jnp.float32)
        return placed.astype(jnp.bfloat16)

    across, along = {}, {}
    last = {r: [] for r in range(planes)}

    def own(r):
        if r:
            row_far[r].wait_recv()
        mine = keys.at[r, 0]
        across[r] = send(mine, keys.at[r, member(0, 0, 1)], peer(0, 0, 1))
        along[r] = [
            send(mine, keys.at[r, member(ys - d, 0, 0)], peer(d, 0, 0)) for d in range(1, ys)
        ]
        last[r].append(send(mine, keys.at[r, member(0, 1, 0)], peer(0, 1, 0)))
        first = (planes - 1 - r) * cap
        queries[first:first + cap, :] = mine[...]

    diagonal = {}

    def forward(r):
        across[r].wait_recv()
        side = keys.at[r, member(0, 0, 1)]
        turned = [
            send(side.at[lower], keys.at[r, member(ys - d, 0, 1)].at[lower], peer(d, 0, 0))
            for d in range(1, ys)
        ]
        last[r].append(send(side, keys.at[r, member(0, 1, 1)], peer(0, 1, 0)))
        crossed = []
        for d in range(1, ys):
            along[r][d - 1].wait_recv()
            side = keys.at[r, member(ys - d, 0, 0)]
            crossed.append(
                send(side.at[upper], keys.at[r, member(ys - d, 0, 1)].at[upper], peer(0, 0, 1))
            )
            last[r].append(send(side, keys.at[r, member(ys - d, 1, 0)], peer(0, 1, 0)))
        diagonal[r] = turned + crossed

    tail = {r: [] for r in range(planes)}

    def share(r):
        for copy in diagonal[r]:
            copy.wait_recv()
        for d in range(1, ys):
            tail[r].append(
                send(keys.at[r, member(ys - d, 0, 1)], keys.at[r, member(ys - d, 1, 1)], peer(0, 1, 0))
            )

    def finish(copies_in):
        for copy in copies_in:
            copy.wait_recv()

    def step(r, query_from, query_to, member_from=0, member_to=members):
        start, size = query_from * cap, (query_to - query_from) * cap
        mine = pl.ds(start, size)
        block = keys[r, member_from:member_to].reshape((member_to - member_from) * cap, width)
        scores = lax.dot_general(
            queries[mine, :], block, (((1,), (1,)), ((), ())), preferred_element_type=jnp.float32
        )
        key_ids = jnp.concatenate([ids[p, r][:, :cap] for p in range(member_from, member_to)], axis=1)
        other = jnp.where(key_ids < 0, NEVER, -penalty * LOG2E)
        bias = jnp.where(query_ids[mine, :] == key_ids, 0.0, other)
        scores = scores * (score_scale * LOG2E / math.sqrt(width)) + bias
        spot = planes - 1 - r
        if member_from == 0 and query_from <= spot < query_to:
            head = scores[:, :lanes]
            lane = iota((size, lanes), 1)
            itself = (iota((size, lanes), 0) - (spot * cap - start) == lane) & (lane < cap)
            scores = jnp.concatenate([jnp.where(itself, NEVER, head), scores[:, lanes:]], axis=1)
        old = peak[mine, :]
        new = jnp.maximum(old, jnp.max(scores, axis=1, keepdims=True))
        shrink = jnp.exp2(old - new)
        weights = jnp.exp2(scores - new)
        total[mine, :] = total[mine, :] * shrink + jnp.sum(weights, axis=1, keepdims=True)
        peak[mine, :] = new
        acc[mine, :] = acc[mine, :] * shrink + jnp.dot(
            weights.astype(jnp.bfloat16), block, preferred_element_type=jnp.float32
        )

    for r in range(planes):
        lane = iota((rows, lanes), 1)
        here = (lane + r * cap == slot_col) & (lane < cap)
        row = jnp.sum(jnp.where(here, cluster_col + 1, 0), axis=0, keepdims=True) - 1
        out_ids[r] = row
        if r == 0:
            ids[0, 0] = row

    id_far = [send(out_ids.at[r], ids.at[0, r], far(r)) for r in range(1, planes)]
    row_far = [None] * planes
    for r in [*range(2, planes), 1]:
        outgoing[r] = place(r)
        row_far[r] = send(outgoing.at[r], keys.at[r, 0], far(r))
    keys[0, 0] = place(0)
    own(0)
    acc[...] = jnp.zeros_like(acc)
    peak[...] = jnp.zeros_like(peak)
    total[...] = jnp.ones_like(total)
    finish(id_far)
    id_near = [
        send(ids.at[0], ids.at[member((ys - dy) % ys, dc, ds)], peer(dy, dc, ds))
        for dy, dc, ds in everyone
    ]
    for r in range(planes):
        first = (planes - 1 - r) * cap
        pick = iota((cap, lanes), 0) == iota((cap, lanes), 1)
        query_ids[first:first + cap, :] = jnp.sum(
            jnp.where(pick, ids[0, r], 0), axis=1, keepdims=True
        )
    final, middle = planes - 1, planes // 2
    forward(0)
    own(1)
    share(0)
    finish(id_near)
    for r in range(2, planes):
        own(r)
        forward(r - 1)
        if r == middle:
            finish(last[0] + tail[0])
            step(0, middle, planes)
        if r > 2:
            share(r - 2)
    step(0, 0, middle)
    for k in range(1, final - 1):
        finish(last[k] + tail[k])
        step(k, middle, planes)
        if k == 1:
            forward(final)
        step(k, 0, middle)
    share(final - 1)
    finish(last[final - 1] + tail[final - 1])
    step(final - 1, middle, planes)
    share(final)
    step(final - 1, 0, middle)
    finish(last[final] + tail[final])

    returned = [None] * planes
    for spot in range(planes):
        if spot == 0:
            step(final, 0, middle)
        elif spot == middle:
            step(final, middle, planes)
        r = final - spot
        first = spot * cap
        sums = total[first:first + cap, :]
        results[r] = (acc[first:first + cap, :] / sums).astype(jnp.bfloat16)
        mass = peak[first:first + cap, :] * LN2 + jnp.log(sums)
        pick = iota((cap, lanes), 0) == iota((cap, lanes), 1)
        masses[r] = jnp.sum(jnp.where(pick, mass, 0.0), axis=0, keepdims=True)
        if r:
            returned[r] = [
                send(results.at[r], back.at[r], far(r)), send(masses.at[r], back_mass.at[r], far(r))
            ]
    found = jnp.zeros((rows, width), jnp.float32)
    mass = jnp.zeros((rows, 1), jnp.float32)
    for r in range(planes):
        lane = iota((rows, lanes), 1)
        here = (lane + r * cap == slot_col) & (lane < cap)
        fetch = (iota((rows, cap), 1) + r * cap == slot_col).astype(jnp.bfloat16)
        if r:
            finish(returned[r])
            block, block_mass = back[r], back_mass[r]
        else:
            block, block_mass = results[0], masses[0]
        found = found + jnp.dot(fetch, block, preferred_element_type=jnp.float32)
        mass = mass + jnp.sum(jnp.where(here, block_mass, 0.0), axis=1, keepdims=True)
    out_ref[...] = found.astype(jnp.bfloat16)
    mass_ref[...] = jnp.sum(jnp.where(eye, mass, 0.0), axis=0, keepdims=True)
    for copy in copies:
        copy.wait_send()


def per_device(embeddings, clusters, cluster_owner):
    rows, width = embeddings.shape
    group_size = lax.axis_size("group")
    tiles = lax.axis_size("tile")
    planes = tiles // SUB
    assert planes == group_size and planes & (planes - 1) == 0
    most = 3 * rows // (2 * group_size)
    cap = -(-most // 16) * 16
    lanes = -(-cap // 128) * 128
    members = group_size * SUB
    slots = planes * cap
    ys = group_size // 2
    count = 3 * (planes - 1) + planes - 1 + members - 1 + planes * (2 + ys - 1 + 4 * (ys - 1) + 1 + ys)
    vmem = pl.BlockSpec(memory_space=pltpu.VMEM)
    out, mass = pl.pallas_call(
        functools.partial(kernel, planes, group_size, cap, lanes),
        out_shape=(
            jax.ShapeDtypeStruct((rows, width), jnp.bfloat16),
            jax.ShapeDtypeStruct((1, rows), jnp.float32),
        ),
        in_specs=[vmem, vmem, pl.BlockSpec(memory_space=pltpu.SMEM)],
        out_specs=(vmem, vmem),
        scratch_shapes=[
            pltpu.VMEM((planes, members, cap, width), jnp.bfloat16),
            pltpu.VMEM((members, planes, 1, lanes), jnp.int32),
            pltpu.VMEM((slots, width), jnp.bfloat16),
            pltpu.VMEM((slots, 1), jnp.int32),
            pltpu.VMEM((slots, width), jnp.float32),
            pltpu.VMEM((slots, 1), jnp.float32),
            pltpu.VMEM((slots, 1), jnp.float32),
            pltpu.VMEM((planes, cap, width), jnp.bfloat16),
            pltpu.VMEM((planes, 1, lanes), jnp.int32),
            pltpu.VMEM((planes, cap, width), jnp.bfloat16),
            pltpu.VMEM((planes, 1, lanes), jnp.float32),
            pltpu.VMEM((planes, cap, width), jnp.bfloat16),
            pltpu.VMEM((planes, 1, lanes), jnp.float32),
            pltpu.SemaphoreType.DMA((count,)),
            pltpu.SemaphoreType.DMA((count,)),
        ],
        compiler_params=pltpu.CompilerParams(
            collective_id=0, has_side_effects=True, vmem_limit_bytes=48 * 1024 * 1024
        ),
    )(embeddings, clusters.reshape(1, rows), cluster_owner)
    return out, mass.reshape(rows)


def solution(mesh):
    placed = (P(("group", "tile"), None), P(("group", "tile")), P())
    return jax.shard_map(
        per_device,
        mesh=mesh,
        in_specs=placed,
        out_specs=(P(("group", "tile"), None), P(("group", "tile"))),
        check_vma=False,
    )
```
